256 devices in a mesh: row: 16 (over y, z_lo), col: 16 (over x, z_hi, core).
Axes of the slice: x: 4, y: 4, z: 8 (z_hi: 2, z_lo: 4; z = z_hi * 4 + z_lo), core: 2. Of those that a mesh axis runs over, the one named last changes fastest.
Arguments:
- tokens: bfloat16 [2048, 4096], P('row', 'col'), may hold values from -6 to 6
- cotangent: bfloat16 [2048, 4096], P('row', 'col'), may hold values from -6 to 6
- gate_weight: bfloat16 [4096, 14336], P('row', 'col'), may hold values from -0.125 to 0.125
- up_weight: bfloat16 [4096, 14336], P('row', 'col'), may hold values from -0.125 to 0.125
- down_weight: bfloat16 [14336, 4096], P('col', 'row'), may hold values from -0.0625 to 0.0625
- gate_mask: int32 [32, 112], P(None, 'col'), may hold values from 0 to 1, as said below
- up_mask: int32 [32, 112], P(None, 'col'), may hold values from 0 to 1, as said below
- down_mask: int32 [112, 32], P('col'), may hold values from 0 to 1, as said below
Outputs:
- output: bfloat16 [2048, 4096], P('row', 'col')
- input_grad: bfloat16 [2048, 4096], P('row', 'col')
- gate_grad: bfloat16 [4096, 14336], P('row', 'col')
- up_grad: bfloat16 [4096, 14336], P('row', 'col')
- down_grad: bfloat16 [14336, 4096], P('col', 'row')
The draws below stay inside these ranges and needn't reach their ends.
Inputs may be any that keep to these rules, and one draw needn't show every extreme that they name: `gate_mask`: blocks of 2 x 7 aligned with the tiles of one device hold between 5 and 7 ones each, and some tile holds exactly 7. `up_mask`: blocks of 2 x 7 aligned with the tiles of one device hold between 5 and 7 ones each, and some tile holds exactly 7. `down_mask`: blocks of 7 x 2 aligned with the tiles of one device hold between 5 and 7 ones each, and some tile holds exactly 7.
All inputs are finite; a program needn't handle non-finite values.
Results may differ from the reference program's by a relative error of at most 0.017.
Values may be sent and summed in bfloat16 or wider, within the bound.
No kernel may reach another device: no remote copies, remote signals or barrier semaphores. Data moves between devices by JAX's collectives and lax.ppermute only.
A program may use at most 128 MiB of HBM per device.

```python
import jax
import jax.numpy as jnp
from jax import lax

D = 4096
FF = 14336
BLK = 128
TOKENS = 2048
TILE_R = 2
TILE_C = 7
N_ROW = 16
N_COL = 16


def tile_mask(key, tile_rows, tile_cols, grid_rows, grid_cols):
    capacity = tile_rows * tile_cols // 2
    tiles_total = grid_rows * grid_cols
    cells = tile_rows * tile_cols
    key_count, key_pick, key_score = jax.random.split(key, 3)
    counts = capacity - jax.random.randint(key_count, (tiles_total,), 0, 3)
    picked = jax.random.randint(key_pick, (), 0, tiles_total)
    counts = jnp.where(jnp.arange(tiles_total) == picked, capacity, counts)
    scores = jax.random.randint(key_score, (tiles_total, cells), 0, 1 << 20) * 1024 + jnp.arange(cells)[None, :]
    order_rank = jnp.argsort(jnp.argsort(scores, axis=1), axis=1)
    masked = (order_rank < counts[:, None]).astype(jnp.int32)
    masked = masked.reshape(grid_rows, grid_cols, tile_rows, tile_cols).transpose(0, 2, 1, 3)
    return masked.reshape(grid_rows * tile_rows, grid_cols * tile_cols)


def draw_gate_mask(key, part):
    key = jax.random.fold_in(key, 11)
    return tile_mask(key, TILE_R, TILE_C, N_ROW, N_COL)


def draw_up_mask(key, part):
    key = jax.random.fold_in(key, 23)
    return tile_mask(key, TILE_R, TILE_C, N_ROW, N_COL)


def draw_down_mask(key, part):
    key = jax.random.fold_in(key, 37)
    return tile_mask(key, TILE_C, TILE_R, N_COL, N_ROW)


def shard_levels(stream_key, shape, shards, low, largest):
    gain, own = 1.0, jax.random.fold_in(stream_key, 6)
    for axis_at, parts in shards:
        steps = jnp.exp(jax.random.uniform(jax.random.fold_in(own, axis_at), (parts,), jnp.float32, low / len(shards), largest / len(shards)))
        gain = gain * jnp.repeat(steps, shape[axis_at] // parts).reshape([-1 if axis == axis_at else 1 for axis in range(len(shape))])
    return gain


def normal_values(key, shape, deviation, most, cuts=(), held_as=jnp.bfloat16):
    entries = deviation * jax.random.normal(key, shape, jnp.float32)
    if cuts:
        entries = entries * shard_levels(key, shape, cuts, -0.22, 0.18)
    return jnp.clip(entries, -most, most).astype(held_as)


def setup_inputs(seed: int = 0) -> dict:
    splits = jax.random.split(jax.random.key(seed), 9)
    tokens = normal_values(splits[0], (TOKENS, D), 1.0, 6.0, ((0, 16), (1, 16)))
    cotangent = normal_values(splits[1], (TOKENS, D), 1.0, 6.0, ((0, 16), (1, 16)))
    gate_weight = normal_values(splits[2], (D, FF), (D // 2) ** -0.5, 0.125, ((0, 16), (1, 16)))
    up_weight = normal_values(splits[3], (D, FF), (D // 2) ** -0.5, 0.125, ((0, 16), (1, 16)))
    down_weight = normal_values(splits[4], (FF, D), (FF // 2) ** -0.5, 0.0625, ((0, 16), (1, 16)))
    gate_mask = draw_gate_mask(jax.random.fold_in(splits[8], 71), 0)
    up_mask = draw_up_mask(jax.random.fold_in(splits[8], 71), 0)
    down_mask = draw_down_mask(jax.random.fold_in(splits[8], 71), 0)
    return {"tokens": tokens, "cotangent": cotangent, "gate_weight": gate_weight, "up_weight": up_weight, "down_weight": down_weight, "gate_mask": gate_mask, "up_mask": up_mask, "down_mask": down_mask}


def spread(mask_blocks):
    return jnp.repeat(jnp.repeat(mask_blocks, BLK, axis=0), BLK, axis=1).astype(jnp.bfloat16)


def reference(tokens, cotangent, gate_weight, up_weight, down_weight, gate_mask, up_mask, down_mask):
    gate_spread = spread(gate_mask)
    up_spread = spread(up_mask)
    down_spread = spread(down_mask)
    gate_eff = gate_weight * gate_spread
    up_eff = up_weight * up_spread
    down_eff = down_weight * down_spread
    gate = jnp.dot(tokens, gate_eff, preferred_element_type=jnp.float32)
    up = jnp.dot(tokens, up_eff, preferred_element_type=jnp.float32)
    sig = jax.nn.sigmoid(gate)
    silu_gate = gate * sig
    hidden = (silu_gate * up).astype(jnp.bfloat16)
    group_width = FF // N_COL

    def out_group(index, total):
        start = (index * group_width).astype(jnp.int32)
        hid_part = lax.dynamic_slice_in_dim(hidden, start, group_width, 1)
        down_part = lax.dynamic_slice_in_dim(down_eff, start, group_width, 0)
        piece = jnp.dot(hid_part, down_part, preferred_element_type=jnp.float32).astype(jnp.bfloat16)
        piece = lax.optimization_barrier(piece)
        return total + piece.astype(jnp.float32)

    output = lax.fori_loop(0, N_COL, out_group, jnp.zeros((TOKENS, D), jnp.float32)).astype(jnp.bfloat16)
    hidden_grad = jnp.dot(cotangent, down_eff.T, preferred_element_type=jnp.float32)
    gate_act_grad = (hidden_grad * up * sig * (1.0 + gate * (1.0 - sig))).astype(jnp.bfloat16)
    up_act_grad = (hidden_grad * silu_gate).astype(jnp.bfloat16)

    def grad_group(index, total):
        start = (index * group_width).astype(jnp.int32)
        gate_part = lax.dynamic_slice_in_dim(gate_act_grad, start, group_width, 1)
        up_part = lax.dynamic_slice_in_dim(up_act_grad, start, group_width, 1)
        gate_cols = lax.dynamic_slice_in_dim(gate_eff, start, group_width, 1)
        up_cols = lax.dynamic_slice_in_dim(up_eff, start, group_width, 1)
        piece = jnp.dot(gate_part, gate_cols.T, preferred_element_type=jnp.float32)
        piece = piece + jnp.dot(up_part, up_cols.T, preferred_element_type=jnp.float32)
        piece = lax.optimization_barrier(piece.astype(jnp.bfloat16))
        return total + piece.astype(jnp.float32)

    input_grad = lax.fori_loop(0, N_COL, grad_group, jnp.zeros((TOKENS, D), jnp.float32)).astype(jnp.bfloat16)
    gate_grad = (jnp.dot(tokens.T, gate_act_grad, preferred_element_type=jnp.float32) * gate_spread).astype(jnp.bfloat16)
    up_grad = (jnp.dot(tokens.T, up_act_grad, preferred_element_type=jnp.float32) * up_spread).astype(jnp.bfloat16)
    down_grad = (jnp.dot(hidden.T, cotangent, preferred_element_type=jnp.float32) * down_spread).astype(jnp.bfloat16)
    return (output, input_grad, gate_grad, up_grad, down_grad)
```

```python
import jax
import jax.numpy as jnp
from jax import lax
from jax.experimental import pallas as pl
from jax.experimental.pallas import tpu as pltpu
from jax.sharding import Mesh, PartitionSpec as P

B = 128
VM = pl.BlockSpec(memory_space=pltpu.VMEM)
SM = pl.BlockSpec(memory_space=pltpu.SMEM)
BF = jnp.bfloat16
F32 = jnp.float32


def sds(shape, dtype=BF):
    return jax.ShapeDtypeStruct(shape, dtype)


def call(kernel, specs, args, outs, scratch=(), flops=0, mib=40):
    nbytes = sum(a.size * a.dtype.itemsize for a in list(args) + list(outs))
    return pl.pallas_call(
        kernel,
        out_shape=tuple(outs),
        in_specs=[SM if s else VM for s in specs],
        out_specs=tuple(VM for _ in outs),
        scratch_shapes=list(scratch),
        compiler_params=pltpu.CompilerParams(vmem_limit_bytes=mib * 1024 * 1024),
        cost_estimate=pl.CostEstimate(flops=flops, bytes_accessed=nbytes, transcendentals=0),
    )(*args)


def cells(mask, tile, down):
    slot = jnp.int32(0)
    for cc in range(7):
        for rr in range(2):
            on = mask[cc, 2 * tile + rr] if down else mask[2 * tile + rr, cc]
            yield rr, cc, on == 1, jnp.minimum(slot, 6)
            slot = slot + on
    yield None, None, slot, None


def sub(rr, cc, down):
    a, b = (cc, rr) if down else (rr, cc)
    return pl.ds(a * B, B), pl.ds(b * B, B)


def pack(mask, tile, down, source, out, base):
    for rr, cc, on, slot in cells(mask, tile, down):
        if rr is None:
            for p in range(5, 7):

                @pl.when(on <= p)
                def _(p=p):
                    out[base + p] = jnp.zeros((B, B), out.dtype)

        else:

            @pl.when(on)
            def _(rr=rr, cc=cc, slot=slot):
                out[base + slot] = source[sub(rr, cc, down)].astype(out.dtype)


def unpack(mask, tile, down, block, store):
    for rr, cc, on, slot in cells(mask, tile, down):
        if rr is not None:
            found = block(slot)
            store(rr, cc, jnp.where(on, found, jnp.zeros_like(found)))


def k_pack(pos, gm, um, dm, gw, uw, dw, gu, dn):
    tile = pos[0] * 4 + pos[1]
    pack(gm, tile, False, gw, gu, 0)
    pack(um, tile, False, uw, gu, 7)
    pack(dm, tile, True, dw, dn, 0)


def k_gate_up(pos, gm, um, p0, p1, p2, p3, full, o0, o1, o2, o3, wg, wu, tok, acc):
    y, z = pos[0], pos[1]
    for j, panel in enumerate((p0, p1, p2, p3)):
        zz = jnp.bitwise_xor(z, j)
        for mask, base, dense in ((gm, 0, wg), (um, 7, wu)):

            def store(rr, cc, v, dense=dense, zz=zz):
                rows = pl.ds(pl.multiple_of(zz * 256 + rr * B, B), B)
                dense[rows, pl.ds(cc * B, B)] = v

            unpack(mask, 4 * y + zz, False, lambda s, base=base, panel=panel: panel[base + s], store)
    for x in range(4):
        for q in range(4):
            tok[x * B : (x + 1) * B, q * 256 : (q + 1) * 256] = full[q % 2, x, q // 2, 0]
    for half, dense in enumerate((wg, wu)):
        got = jnp.dot(tok[...], dense[...], preferred_element_type=F32)
        acc[:, :, half * 896 : (half + 1) * 896] = got.reshape(4, B, 896)
    o0[...] = acc[y]
    for j, out in ((1, o1), (2, o2), (3, o3)):
        out[...] = acc[jnp.bitwise_xor(y, j)].astype(BF)


def k_hidden_grad(pos, dm, p0, p1, p2, p3, full, o0, o1, o2, o3, wd, cot, acc):
    y, z = pos[0], pos[1]
    for j, panel in enumerate((p0, p1, p2, p3)):
        zz = jnp.bitwise_xor(z, j)

        def store(rr, cc, v, zz=zz):
            wd[zz, pl.ds(cc * B, B), pl.ds(rr * B, B)] = v

        unpack(dm, 4 * y + zz, True, lambda s, panel=panel: panel[s], store)
    for x in range(4):
        for q in range(4):
            cot[x * B : (x + 1) * B, q * 256 : (q + 1) * 256] = full[q % 2, x, q // 2, 1]
    got = None
    for q in range(4):
        term = lax.dot_general(
            cot[:, q * 256 : (q + 1) * 256],
            wd[q],
            (((1,), (1,)), ((), ())),
            preferred_element_type=F32,
        )
        got = term if got is None else got + term
    acc[...] = got.reshape(4, B, 896)
    o0[...] = acc[y]
    for j, out in ((1, o1), (2, o2), (3, o3)):
        out[...] = acc[jnp.bitwise_xor(y, j)].astype(BF)


def total(own, *others):
    out = own[...]
    for o in others:
        out = out + o[...].astype(F32)
    return out


def k_hidden(a0, a1, a2, a3, hid):
    both = total(a0, a1, a2, a3)
    gate, up = both[:, :896], both[:, 896:]
    hid[...] = (gate * jax.nn.sigmoid(gate) * up).astype(BF)


def k_act(a0, a1, a2, a3, b0, b1, b2, b3, act):
    both = total(a0, a1, a2, a3)
    gate, up = both[:, :896], both[:, 896:]
    grad = total(b0, b1, b2, b3)
    sig = jax.nn.sigmoid(gate)
    act[:, :896] = (grad * up * sig * (1.0 + gate * (1.0 - sig))).astype(BF)
    act[:, 896:] = (grad * (gate * sig)).astype(BF)


def columns(q):
    return pl.ds(pl.multiple_of(q * 256, 256), 256)


TN = (((0,), (0,)), ((), ()))
NT = (((1,), (1,)), ((), ()))


def k_down_grad(pos, dm, h0, h1, h2, h3, cot, d0, d1, d2, d3, hid, acc):
    y, z = pos[0], pos[1]
    for j, h in enumerate((h0, h1, h2, h3)):
        hid[jnp.bitwise_xor(y, j)] = h[...]
    left = hid[...].reshape(512, 896)
    for j, out in ((1, d1), (2, d2), (3, d3), (0, d0)):
        zz = jnp.bitwise_xor(z, j)
        acc[...] = lax.dot_general(left, cot[:, columns(zz)], TN, preferred_element_type=F32)
        pack(dm, 4 * y + zz, True, acc, out, 0)


def k_weight_grad(pos, gm, um, a0, a1, a2, a3, tok, d0, d1, d2, d3, act, acc):
    y, z = pos[0], pos[1]
    for j, a in enumerate((a0, a1, a2, a3)):
        act[jnp.bitwise_xor(y, j)] = a[...]
    right = act[...].reshape(512, 1792)
    for j, out in ((1, d1), (2, d2), (3, d3), (0, d0)):
        zz = jnp.bitwise_xor(z, j)
        got = lax.dot_general(tok[:, columns(zz)], right, TN, preferred_element_type=F32)
        acc[0] = got[:, :896]
        acc[1] = got[:, 896:]
        pack(gm, 4 * y + zz, False, acc.at[0], out, 0)
        pack(um, 4 * y + zz, False, acc.at[1], out, 7)


def k_out(pos, hid, wd, keep, send):
    k = pos[4]
    left = hid[...].reshape(512, 896)
    for out, kk in ((send, 1 - k), (keep, k)):
        for h in range(2):
            got = jnp.dot(left, wd[2 * h + kk], preferred_element_type=F32)
            out[:, h] = got.reshape(4, B, 256).astype(out.dtype)


def k_in(pos, act, wg, wu, keep, send):
    k = pos[4]
    both = act[...].reshape(512, 1792)
    left, right = both[:, :896], both[:, 896:]
    for out, kk in ((send, 1 - k), (keep, k)):
        for h in range(2):
            rows = columns(2 * h + kk)
            got = lax.dot_general(left, wg[rows, :], NT, preferred_element_type=F32)
            got = got + lax.dot_general(right, wu[rows, :], NT, preferred_element_type=F32)
            out[:, h] = got.reshape(4, B, 256).astype(out.dtype)


def k_sum_core(pos, keep, got, o0, o1, o2, o3):
    x = pos[2]
    for j, out in enumerate((o0, o1, o2, o3)):
        at = jnp.bitwise_xor(x, j)
        out[...] = (keep[at] + got[at].astype(F32)).astype(out.dtype)


def k_sum_x(pos, a0, a1, a2, a3, keep, send, acc):
    h = pos[3]
    acc[...] = total(a0, a1, a2, a3)
    keep[...] = acc[h]
    send[...] = acc[1 - h].astype(BF)


def k_sum_pair(a, b, out):
    out[...] = (a[...] + b[...].astype(F32)).astype(BF)


def k_place(pos, mask, a0, a1, a2, a3, out, *, base, down):
    tile = pos[0] * 4 + pos[1]

    def block(s):
        return total(a0.at[base + s], a1.at[base + s], a2.at[base + s], a3.at[base + s])

    def store(rr, cc, v):
        out[sub(rr, cc, down)] = v.astype(BF)

    unpack(mask, tile, down, block, store)


def exchange(value, axis, by, size=4):
    return lax.ppermute(value, axis, [(i, i ^ by) for i in range(size)])


def spread(value, axis):
    return [value] + [exchange(value, axis, j) for j in (1, 2, 3)]


def collect(own, others, axis):
    return [own] + [exchange(v, axis, j) for j, v in zip((1, 2, 3), others)]


def swap(value):
    pairs = [(y * 4 + x, x * 4 + y) for y in range(4) for x in range(4)]
    return lax.ppermute(value, ("y", "x"), pairs)


def scatter_sum(pos, keep, send):
    got = exchange(send, "k", 1, 2)
    part = (2, B, 256)
    s = call(
        k_sum_core, (1, 0, 0), (pos, keep, got),
        (sds(part, F32), sds(part), sds(part), sds(part)),
    )
    own, other = call(
        k_sum_x, (1, 0, 0, 0, 0), (pos, *collect(s[0], s[1:], "x")),
        (sds((B, 256), F32), sds((B, 256))), (pltpu.VMEM(part, F32),),
    )
    (done,) = call(k_sum_pair, (0, 0), (own, exchange(other, "h", 1, 2)), (sds((B, 256)),))
    return swap(done)


def body(tokens, cotangent, gate_weight, up_weight, down_weight, gate_mask, up_mask, down_mask):
    pos = jnp.stack([lax.axis_index(a) for a in ("y", "z", "x", "h", "k")]).astype(jnp.int32)
    masks = (gate_mask, up_mask, down_mask)
    both = swap(jnp.stack([tokens, cotangent]))
    gu, dn = call(
        k_pack, (1, 1, 1, 1, 0, 0, 0),
        (pos, *masks, gate_weight, up_weight, down_weight),
        (sds((14, B, B)), sds((7, B, B))),
    )
    gu_all = spread(gu, "z")
    dn_all = spread(dn, "z")
    full = both
    for axis in ("h", "x", "k"):
        full = lax.all_gather(full, axis, axis=0)
    blk = (B, 1792)
    g = call(
        k_gate_up, (1, 1, 1, 0, 0, 0, 0, 0), (pos, gate_mask, up_mask, *gu_all, full),
        (sds(blk, F32), sds(blk), sds(blk), sds(blk),
         sds((1024, 896)), sds((1024, 896)), sds((512, 1024))),
        (pltpu.VMEM((4, B, 1792), F32),), flops=2 * 512 * 1024 * 1792,
    )
    wg, wu, tok = g[4:]
    g_all = collect(g[0], g[1:4], "y")
    blk = (B, 896)
    d = call(
        k_hidden_grad, (1, 1, 0, 0, 0, 0, 0), (pos, down_mask, *dn_all, full),
        (sds(blk, F32), sds(blk), sds(blk), sds(blk), sds((4, 896, 256)), sds((512, 1024))),
        (pltpu.VMEM((4, B, 896), F32),), flops=2 * 512 * 1024 * 896,
    )
    wd, cot = d[4:]
    d_all = collect(d[0], d[1:4], "y")
    (hidden,) = call(k_hidden, (0,) * 4, g_all, (sds((B, 896)),))
    hid_all = spread(hidden, "y")
    (act,) = call(k_act, (0,) * 8, (*g_all, *d_all), (sds((B, 1792)),))
    act_all = spread(act, "y")
    blk = (7, B, B)
    e = call(
        k_down_grad, (1, 1, 0, 0, 0, 0, 0), (pos, down_mask, *hid_all, cot),
        (sds(blk, F32), sds(blk), sds(blk), sds(blk), sds((4, B, 896))),
        (pltpu.VMEM((896, 256), F32),), flops=2 * 512 * 1024 * 896,
    )
    e_all = collect(e[0], e[1:4], "z")
    half = (4, 2, B, 256)
    keep, send = call(
        k_out, (1, 0, 0), (pos, e[4], wd), (sds(half, F32), sds(half)),
        flops=2 * 512 * 1024 * 896,
    )
    output = scatter_sum(pos, keep, send)
    blk = (14, B, B)
    f = call(
        k_weight_grad, (1, 1, 1, 0, 0, 0, 0, 0), (pos, gate_mask, up_mask, *act_all, tok),
        (sds(blk, F32), sds(blk), sds(blk), sds(blk), sds((4, B, 1792))),
        (pltpu.VMEM((2, 256, 896), F32),), flops=2 * 512 * 1024 * 1792,
    )
    f_all = collect(f[0], f[1:4], "z")
    keep, send = call(
        k_in, (1, 0, 0, 0), (pos, f[4], wg, wu), (sds(half, F32), sds(half)),
        flops=2 * 512 * 1024 * 1792,
    )
    input_grad = scatter_sum(pos, keep, send)

    def place(mask, parts, base, down, shape):
        def kernel(*refs):
            k_place(*refs, base=base, down=down)

        return call(kernel, (1, 1, 0, 0, 0, 0), (pos, mask, *parts), (sds(shape),))[0]

    down_grad = place(down_mask, e_all, 0, True, (896, 256))
    gate_grad = place(gate_mask, f_all, 0, False, (256, 896))
    up_grad = place(up_mask, f_all, 7, False, (256, 896))
    return (output, input_grad, gate_grad, up_grad, down_grad)


def solution(mesh):
    mesh = Mesh(mesh.devices.reshape(4, 4, 4, 2, 2), ("y", "z", "x", "h", "k"))
    row, col = ("y", "z"), ("x", "h", "k")
    return jax.shard_map(
        body,
        mesh=mesh,
        in_specs=(
            P(row, col),
            P(row, col),
            P(row, col),
            P(row, col),
            P(col, row),
            P(None, col),
            P(None, col),
            P(col, None),
        ),
        out_specs=(P(row, col), P(row, col), P(row, col), P(row, col), P(col, row)),
        check_vma=False,
    )
```

```python
import jax
import jax.numpy as jnp
from jax import lax
from jax.experimental import pallas as pl
from jax.experimental.pallas import tpu as pltpu
from jax.sharding import Mesh, PartitionSpec as P

B = 128
VM = pl.BlockSpec(memory_space=pltpu.VMEM)
SM = pl.BlockSpec(memory_space=pltpu.SMEM)
BF = jnp.bfloat16
F32 = jnp.float32


def sds(shape, dtype=BF):
    return jax.ShapeDtypeStruct(shape, dtype)


def call(kernel, specs, args, outs, scratch=(), flops=0, mib=24):
    nbytes = sum(a.size * a.dtype.itemsize for a in list(args) + list(outs))
    return pl.pallas_call(
        kernel,
        out_shape=tuple(outs),
        in_specs=[(VM, SM, pl.BlockSpec(memory_space=pltpu.HBM))[s] for s in specs],
        out_specs=tuple(VM for _ in outs),
        scratch_shapes=list(scratch),
        compiler_params=pltpu.CompilerParams(vmem_limit_bytes=mib * 1024 * 1024),
        cost_estimate=pl.CostEstimate(flops=flops, bytes_accessed=nbytes, transcendentals=0),
    )(*args)


def cells(mask, tile, down):
    slot = jnp.int32(0)
    for cc in range(7):
        for rr in range(2):
            on = mask[cc, 2 * tile + rr] if down else mask[2 * tile + rr, cc]
            yield rr, cc, on == 1, jnp.minimum(slot, 6)
            slot = slot + on
    yield None, None, slot, None


def sub(rr, cc, down):
    a, b = (cc, rr) if down else (rr, cc)
    return pl.ds(a * B, B), pl.ds(b * B, B)


def pack(mask, tile, down, source, out):
    for rr, cc, on, slot in cells(mask, tile, down):
        if rr is None:
            for p in range(5, 7):

                @pl.when(on <= p)
                def _(p=p):
                    out[p] = jnp.zeros((B, B), out.dtype)

        else:

            @pl.when(on)
            def _(rr=rr, cc=cc, slot=slot):
                out[slot] = source[sub(rr, cc, down)].astype(out.dtype)


def unpack(mask, tile, down, block, store):
    for rr, cc, on, slot in cells(mask, tile, down):
        if rr is not None:
            found = block(slot)
            store(rr, cc, jnp.where(on, found, jnp.zeros_like(found)))


def k_pack(pos, gm, um, dm, gw, uw, dw, gp, up, dp, gv, uv, dv, sems):
    tile = pos[0] * 4 + pos[1]
    copies = [
        pltpu.make_async_copy(src, dst, sems.at[i])
        for i, (src, dst) in enumerate(((dw, dv), (gw, gv), (uw, uv)))
    ]
    for c in copies:
        c.start()
    copies[0].wait()
    pack(dm, tile, True, dv, dp)
    copies[1].wait()
    pack(gm, tile, False, gv, gp)
    copies[2].wait()
    pack(um, tile, False, uv, up)


def assemble(pos, mine, other, which, out):
    x, h, k = pos[2], pos[3], pos[4]
    for s in range(4):
        rows = pl.ds(pl.multiple_of(jnp.bitwise_xor(x, s) * B, B), B)
        for a in range(2):
            for b, piece in enumerate((mine, other)):
                q = 2 * jnp.bitwise_xor(h, a) + jnp.bitwise_xor(k, b)
                out[rows, columns(q)] = piece[s, a, which]


def dense_tile_rows(y, mask, panel, dense):
    for z in range(4):

        def store(rr, cc, v):
            dense[z * 256 + rr * B : z * 256 + (rr + 1) * B, cc * B : (cc + 1) * B] = v

        unpack(mask, 4 * y + z, False, lambda s: panel[z, s], store)


def shares(y, acc, outs, at=()):
    outs[0][at + (Ellipsis,)] = acc[y]
    for j in (1, 2, 3):
        outs[j][at + (Ellipsis,)] = acc[jnp.bitwise_xor(y, j)].astype(BF)


def k_grad_gate(pos, dm, gm, dp, gp, mine, other, o0, o1, o2, o3, wd, wg, cot, tok, acc):
    y = pos[0]
    for z in range(4):

        def store(rr, cc, v):
            wd[z, cc * B : (cc + 1) * B, rr * B : (rr + 1) * B] = v

        unpack(dm, 4 * y + z, True, lambda s: dp[z, s], store)
    assemble(pos, mine, other, 1, cot)
    got = None
    for q in range(4):
        term = lax.dot_general(
            cot[:, q * 256 : (q + 1) * 256], wd[q], NT, preferred_element_type=F32
        )
        got = term if got is None else got + term
    acc[...] = got.reshape(4, B, 896)
    shares(y, acc, (o0, o1, o2, o3), (0,))
    dense_tile_rows(y, gm, gp, wg)
    assemble(pos, mine, other, 0, tok)
    got = jnp.dot(tok[...], wg[...], preferred_element_type=F32)
    acc[...] = got.reshape(4, B, 896)
    shares(y, acc, (o0, o1, o2, o3), (1,))


def k_up(pos, mask, panel, tok, o0, o1, o2, o3, dense, acc):
    dense_tile_rows(pos[0], mask, panel, dense)
    got = jnp.dot(tok[...], dense[...], preferred_element_type=F32)
    acc[...] = got.reshape(4, B, 896)
    shares(pos[0], acc, (o0, o1, o2, o3))


def total(own, *others):
    out = own[...]
    for o in others:
        out = out + o[...].astype(F32)
    return out


def k_act(a0, a1, a2, a3, b0, b1, b2, b3, hid, act):
    both = total(a0, a1, a2, a3)
    grad, gate = both[0], both[1]
    up = total(b0, b1, b2, b3)
    sig = jax.nn.sigmoid(gate)
    hid[...] = (gate * sig * up).astype(BF)
    act[0] = (grad * up * sig * (1.0 + gate * (1.0 - sig))).astype(BF)
    act[1] = (grad * (gate * sig)).astype(BF)


def columns(q):
    return pl.ds(pl.multiple_of(q * 256, 256), 256)


TN = (((0,), (0,)), ((), ()))
NT = (((1,), (1,)), ((), ()))


def k_down_grad(pos, dm, hid, cot, d0, d1, d2, d3, acc):
    y, z = pos[0], pos[1]
    left = hid[...].reshape(512, 896)
    for j, out in ((1, d1), (2, d2), (3, d3), (0, d0)):
        zz = jnp.bitwise_xor(z, j)
        acc[...] = lax.dot_general(left, cot[:, columns(zz)], TN, preferred_element_type=F32)
        pack(dm, 4 * y + zz, True, acc, out)


def k_weight_grad(pos, gm, um, act, tok, d0, d1, d2, d3, acc):
    y, z = pos[0], pos[1]
    for half, mask in enumerate((gm, um)):
        right = act[:, half].reshape(512, 896)
        for j, out in ((1, d1), (2, d2), (3, d3), (0, d0)):
            zz = jnp.bitwise_xor(z, j)
            acc[...] = lax.dot_general(tok[:, columns(zz)], right, TN, preferred_element_type=F32)
            pack(mask, 4 * y + zz, False, acc, out.at[half])


def k_out(pos, hid, wd, keep, send):
    k = pos[4]
    left = hid[...].reshape(512, 896)
    for out, kk in ((send, 1 - k), (keep, k)):
        for h in range(2):
            got = jnp.dot(left, wd[2 * h + kk], preferred_element_type=F32)
            out[:, h] = got.reshape(4, B, 256).astype(out.dtype)


def k_in(pos, act, wg, wu, keep, send):
    k = pos[4]
    gact, uact = act[:, 0].reshape(512, 896), act[:, 1].reshape(512, 896)
    for out, kk in ((send, 1 - k), (keep, k)):
        for h in range(2):
            rows = columns(2 * h + kk)
            got = lax.dot_general(gact, wg[rows, :], NT, preferred_element_type=F32)
            got = got + lax.dot_general(uact, wu[rows, :], NT, preferred_element_type=F32)
            out[:, h] = got.reshape(4, B, 256).astype(out.dtype)


def k_sum_core(pos, keep, got, o0, o1, o2, o3):
    x = pos[2]
    for j, out in enumerate((o0, o1, o2, o3)):
        at = jnp.bitwise_xor(x, j)
        out[...] = (keep[at] + got[at].astype(F32)).astype(out.dtype)


def k_sum_x(pos, a0, a1, a2, a3, keep, send, acc):
    h = pos[3]
    acc[...] = total(a0, a1, a2, a3)
    keep[...] = acc[h].astype(BF)
    send[...] = acc[1 - h].astype(BF)


def k_sum_x_join(pos, a0, a1, a2, a3, first, second, keep, send, acc):
    h = pos[3]
    acc[...] = total(a0, a1, a2, a3)
    keep[0] = first[...]
    keep[1] = acc[h].astype(BF)
    send[0] = second[...]
    send[1] = acc[1 - h].astype(BF)


def k_sum_pair(a, b, out, grad):
    both = a[...].astype(F32) + b[...].astype(F32)
    out[...] = both[0].astype(BF)
    grad[...] = both[1].astype(BF)


def k_place(pos, mask, a0, a1, a2, a3, out, *, down, at):
    tile = pos[0] * 4 + pos[1]

    def block(s):
        return total(a0.at[at + (s,)], a1.at[at + (s,)], a2.at[at + (s,)], a3.at[at + (s,)])

    def store(rr, cc, v):
        out[sub(rr, cc, down)] = v.astype(BF)

    unpack(mask, tile, down, block, store)


def exchange(value, axis, by, size=4):
    return lax.ppermute(value, axis, [(i, i ^ by) for i in range(size)])


def spread(value, axis):
    return [value] + [exchange(value, axis, j) for j in (1, 2, 3)]


def collect(own, others, axis):
    return [own] + [exchange(v, axis, j) for j, v in zip((1, 2, 3), others)]


def swap(value, flip):
    pairs = [
        ((y * 4 + x) * 2 + h, (x * 4 + y) * 2 + (h ^ flip))
        for y in range(4)
        for x in range(4)
        for h in range(2)
    ]
    return lax.ppermute(value, ("y", "x", "h"), pairs)


def body(tokens, cotangent, gate_weight, up_weight, down_weight, gate_mask, up_mask, down_mask):
    pos = jnp.stack([lax.axis_index(a) for a in ("y", "z", "x", "h", "k")]).astype(jnp.int32)
    masks = (gate_mask, up_mask, down_mask)
    both = jnp.stack([tokens, cotangent])
    pair = jnp.stack([swap(both, 0), swap(both, 1)])
    packed = sds((7, B, B))
    gp, up, dp = call(
        k_pack, (1, 1, 1, 1, 2, 2, 2),
        (pos, *masks, gate_weight, up_weight, down_weight), (packed,) * 3,
        (pltpu.VMEM((256, 896), BF), pltpu.VMEM((256, 896), BF), pltpu.VMEM((896, 256), BF),
         pltpu.SemaphoreType.DMA((3,))),
    )
    dp, pair = lax.optimization_barrier((dp, pair))
    mine = spread(pair, "x")
    dp = lax.all_gather(dp, "z", axis=0)
    gp, dp, mine = lax.optimization_barrier((gp, dp, mine))
    mine = jnp.stack(mine)
    other = exchange(mine, "k", 1, 2)
    gp = lax.all_gather(gp, "z", axis=0)
    acc = pltpu.VMEM((4, B, 896), F32)
    flops = 2 * 512 * 1024 * 896
    blk = (2, B, 896)
    g = call(
        k_grad_gate, (1, 1, 1, 0, 0, 0, 0), (pos, down_mask, gate_mask, dp, gp, mine, other),
        (sds(blk, F32), sds(blk), sds(blk), sds(blk),
         sds((4, 896, 256)), sds((1024, 896)), sds((512, 1024)), sds((512, 1024))),
        (acc,), flops=2 * flops,
    )
    wd, wg, cot, tok = g[4:]
    g_all = collect(g[0], g[1:4], "y")
    up, _ = lax.optimization_barrier((up, g[1]))
    up = lax.all_gather(up, "z", axis=0)
    up, g_all = lax.optimization_barrier((up, g_all))
    blk = (B, 896)
    u = call(
        k_up, (1, 1, 0, 0), (pos, up_mask, up, tok),
        (sds(blk, F32), sds(blk), sds(blk), sds(blk), sds((1024, 896))), (acc,), flops=flops,
    )
    wu = u[4]
    u_all = collect(u[0], u[1:4], "y")
    hidden, act = call(k_act, (0,) * 8, (*g_all, *u_all), (sds(blk), sds((2, B, 896))))
    act = lax.all_gather(act, "y", axis=0)
    hidden = lax.all_gather(hidden, "y", axis=0)
    blk = (7, B, B)
    e = call(
        k_down_grad, (1, 1, 0, 0), (pos, down_mask, hidden, cot),
        (sds(blk, F32), sds(blk), sds(blk), sds(blk)),
        (pltpu.VMEM((896, 256), F32),), flops=flops,
    )
    e_all = collect(e[0], e[1:4], "z")
    half, part, one = (4, 2, B, 256), (2, B, 256), (B, 256)

    def sum_core(keep, got):
        return call(
            k_sum_core, (1, 0, 0), (pos, keep, got),
            (sds(part, F32), sds(part), sds(part), sds(part)),
        )

    hidden, _ = lax.optimization_barrier((hidden, e[1]))
    keep, send = call(
        k_out, (1, 0, 0), (pos, hidden, wd), (sds(half, F32), sds(half)), flops=flops
    )
    got = exchange(send, "k", 1, 2)
    s = sum_core(keep, got)
    s_all = collect(s[0], s[1:], "x")
    own, other = call(
        k_sum_x, (1, 0, 0, 0, 0), (pos, *s_all), (sds(one), sds(one)), (pltpu.VMEM(part, F32),)
    )
    act, e_all, own = lax.optimization_barrier((act, e_all, own))
    keep, send = call(
        k_in, (1, 0, 0, 0), (pos, act, wg, wu), (sds(half, F32), sds(half)), flops=2 * flops
    )
    got = exchange(send, "k", 1, 2)
    act, keep = lax.optimization_barrier((act, keep))
    blk = (2, 7, B, B)
    f = call(
        k_weight_grad, (1, 1, 1, 0, 0), (pos, gate_mask, up_mask, act, tok),
        (sds(blk, F32), sds(blk), sds(blk), sds(blk)),
        (pltpu.VMEM((256, 896), F32),), flops=2 * flops,
    )
    f_all = collect(f[0], f[1:4], "z")
    keep, _ = lax.optimization_barrier((keep, f[1]))
    s = sum_core(keep, got)
    own, other = call(
        k_sum_x_join, (1,) + (0,) * 6, (pos, *collect(s[0], s[1:], "x"), own, other),
        (sds((2, B, 256)), sds((2, B, 256))), (pltpu.VMEM(part, F32),),
    )
    output, input_grad = call(
        k_sum_pair, (0, 0), (swap(own, 0), swap(other, 1)), (sds((B, 256)),) * 2
    )

    def place(mask, parts, down, at, shape):
        def kernel(*refs):
            k_place(*refs, down=down, at=at)

        return call(kernel, (1, 1, 0, 0, 0, 0), (pos, mask, *parts), (sds(shape),))[0]

    down_grad = place(down_mask, e_all, True, (), (896, 256))
    gate_grad = place(gate_mask, f_all, False, (0,), (256, 896))
    up_grad = place(up_mask, f_all, False, (1,), (256, 896))
    return (output, input_grad, gate_grad, up_grad, down_grad)


def solution(mesh):
    mesh = Mesh(mesh.devices.reshape(4, 4, 4, 2, 2), ("y", "z", "x", "h", "k"))
    row, col = ("y", "z"), ("x", "h", "k")
    return jax.shard_map(
        body,
        mesh=mesh,
        in_specs=(
            P(row, col),
            P(row, col),
            P(row, col),
            P(row, col),
            P(col, row),
            P(None, col),
            P(None, col),
            P(col, None),
        ),
        out_specs=(P(row, col), P(row, col), P(row, col), P(row, col), P(col, row)),
        check_vma=False,
    )
```

```python
import jax
import jax.numpy as jnp
from jax import lax
from jax.experimental import pallas as pl
from jax.experimental.pallas import tpu as pltpu
from jax.sharding import Mesh, PartitionSpec as P

B = 128
VM = pl.BlockSpec(memory_space=pltpu.VMEM)
SM = pl.BlockSpec(memory_space=pltpu.SMEM)
BF = jnp.bfloat16
F32 = jnp.float32


def sds(shape, dtype=BF):
    return jax.ShapeDtypeStruct(shape, dtype)


def call(kernel, specs, args, outs, scratch=(), flops=0, mib=24, small=False):
    nbytes = 0 if small else sum(a.size * a.dtype.itemsize for a in list(args) + list(outs))
    return pl.pallas_call(
        kernel,
        out_shape=tuple(outs),
        in_specs=[(VM, SM, pl.BlockSpec(memory_space=pltpu.HBM))[s] for s in specs],
        out_specs=tuple(VM for _ in outs),
        scratch_shapes=list(scratch),
        compiler_params=pltpu.CompilerParams(vmem_limit_bytes=mib and mib * 1024 * 1024),
        cost_estimate=pl.CostEstimate(flops=flops, bytes_accessed=nbytes, transcendentals=0),
    )(*args)


GATE, UP, DOWN = 0, 7, 14


def cells(mask, tile, which):
    slot = jnp.int32(0)
    for cc in range(7):
        for rr in range(2):
            on = mask[which + cc, 2 * tile + rr]
            yield rr, cc, on == 1, jnp.minimum(slot, 6)
            slot = slot + on
    yield None, None, slot, None


def sub(rr, cc, which):
    a, b = (cc, rr) if which == DOWN else (rr, cc)
    return pl.ds(a * B, B), pl.ds(b * B, B)


def pack(mask, tile, which, source, out):
    for rr, cc, on, slot in cells(mask, tile, which):
        if rr is None:
            for p in range(5, 7):

                @pl.when(on <= p)
                def _(p=p):
                    out[p] = jnp.zeros((B, B), out.dtype)

        else:

            @pl.when(on)
            def _(rr=rr, cc=cc, slot=slot):
                out[slot] = source[sub(rr, cc, which)].astype(out.dtype)


def unpack(mask, tile, which, block, store):
    for rr, cc, on, slot in cells(mask, tile, which):
        if rr is not None:
            found = block(slot)
            store(rr, cc, jnp.where(on, found, jnp.zeros_like(found)))


def k_pack(pos, mask, gw, uw, dw, gp, up, dp, gv, uv, dv, sems):
    tile = pos[0] * 4 + pos[1]
    copies = [
        pltpu.make_async_copy(src, dst, sems.at[i])
        for i, (src, dst) in enumerate(((dw, dv), (gw, gv), (uw, uv)))
    ]
    for c in copies:
        c.start()
    copies[0].wait()
    pack(mask, tile, DOWN, dv, dp)
    copies[1].wait()
    pack(mask, tile, GATE, gv, gp)
    copies[2].wait()
    pack(mask, tile, UP, uv, up)


def assemble(pos, mine, other, which, out):
    x, h, k = pos[2], pos[3], pos[4]
    for s in range(4):
        rows = pl.ds(pl.multiple_of(jnp.bitwise_xor(x, s) * B, B), B)
        for a in range(2):
            for b, piece in enumerate((mine, other)):
                q = 2 * jnp.bitwise_xor(h, a) + jnp.bitwise_xor(k, b)
                out[rows, columns(q)] = piece[s, a, which]


def dense_tile_rows(y, mask, which, panel, dense):
    for z in range(4):

        def store(rr, cc, v):
            dense[z * 256 + rr * B : z * 256 + (rr + 1) * B, cc * B : (cc + 1) * B] = v

        unpack(mask, 4 * y + z, which, lambda s: panel[z, s], store)


def shares(y, acc, outs, at=()):
    outs[0][at + (Ellipsis,)] = acc[y]
    for j in (1, 2, 3):
        outs[j][at + (Ellipsis,)] = acc[jnp.bitwise_xor(y, j)].astype(BF)


def k_grad_gate(pos, mask, dp, gp, mine, other, o0, o1, o2, o3, wd, wg, cot, tok, acc):
    y = pos[0]
    for z in range(4):

        def store(rr, cc, v):
            wd[z, cc * B : (cc + 1) * B, rr * B : (rr + 1) * B] = v

        unpack(mask, 4 * y + z, DOWN, lambda s: dp[z, s], store)
    assemble(pos, mine, other, 1, cot)
    got = None
    for q in range(4):
        term = lax.dot_general(
            cot[:, q * 256 : (q + 1) * 256], wd[q], NT, preferred_element_type=F32
        )
        got = term if got is None else got + term
    acc[...] = got.reshape(4, B, 896)
    shares(y, acc, (o0, o1, o2, o3), (0,))
    dense_tile_rows(y, mask, GATE, gp, wg)
    assemble(pos, mine, other, 0, tok)
    got = jnp.dot(tok[...], wg[...], preferred_element_type=F32)
    acc[...] = got.reshape(4, B, 896)
    shares(y, acc, (o0, o1, o2, o3), (1,))


def k_up(pos, mask, panel, tok, o0, o1, o2, o3, dense, acc):
    dense_tile_rows(pos[0], mask, UP, panel, dense)
    got = jnp.dot(tok[...], dense[...], preferred_element_type=F32)
    acc[...] = got.reshape(4, B, 896)
    shares(pos[0], acc, (o0, o1, o2, o3))


def total(own, *others):
    out = own[...]
    for o in others:
        out = out + o[...].astype(F32)
    return out


def k_act(a0, a1, a2, a3, b0, b1, b2, b3, hid, act):
    both = total(a0, a1, a2, a3)
    grad, gate = both[0], both[1]
    up = total(b0, b1, b2, b3)
    sig = jax.nn.sigmoid(gate)
    hid[...] = (gate * sig * up).astype(BF)
    act[0] = (grad * up * sig * (1.0 + gate * (1.0 - sig))).astype(BF)
    act[1] = (grad * (gate * sig)).astype(BF)


def columns(q):
    return pl.ds(pl.multiple_of(q * 256, 256), 256)


TN = (((0,), (0,)), ((), ()))
NT = (((1,), (1,)), ((), ()))


def k_down_grad(pos, mask, hid, cot, d0, d1, d2, d3, acc):
    y, z = pos[0], pos[1]
    left = hid[...].reshape(512, 896)
    for j, out in ((1, d1), (2, d2), (3, d3), (0, d0)):
        zz = jnp.bitwise_xor(z, j)
        acc[...] = lax.dot_general(left, cot[:, columns(zz)], TN, preferred_element_type=F32)
        pack(mask, 4 * y + zz, DOWN, acc, out)


def k_weight_grad(pos, mask, act, tok, d0, d1, d2, d3, acc):
    y, z = pos[0], pos[1]
    for half, which in enumerate((GATE, UP)):
        right = act[half].reshape(512, 896)
        for j, out in ((1, d1), (2, d2), (3, d3), (0, d0)):
            zz = jnp.bitwise_xor(z, j)
            acc[...] = lax.dot_general(tok[:, columns(zz)], right, TN, preferred_element_type=F32)
            pack(mask, 4 * y + zz, which, acc, out.at[half])


def k_out_in(pos, hid, a0, a1, a2, a3, wd, wg, wu, act, keep, send):
    y, k = pos[0], pos[4]
    for j, a in enumerate((a0, a1, a2, a3)):
        for half in range(2):
            act[half, jnp.bitwise_xor(y, j)] = a[half]
    left = hid[...].reshape(512, 896)
    gact, uact = act[0].reshape(512, 896), act[1].reshape(512, 896)
    for out, kk in ((send, 1 - k), (keep, k)):
        for h in range(2):
            q = 2 * h + kk
            got = jnp.dot(left, wd[q], preferred_element_type=F32)
            out[:, 0, h] = got.reshape(4, B, 256).astype(out.dtype)
            rows = columns(q)
            got = lax.dot_general(gact, wg[rows, :], NT, preferred_element_type=F32)
            got = got + lax.dot_general(uact, wu[rows, :], NT, preferred_element_type=F32)
            out[:, 1, h] = got.reshape(4, B, 256).astype(out.dtype)


def k_sum_core(pos, keep, got, o0, o1, o2, o3):
    x = pos[2]
    for j, out in enumerate((o0, o1, o2, o3)):
        at = jnp.bitwise_xor(x, j)
        out[...] = (keep[at] + got[at].astype(F32)).astype(out.dtype)


def k_sum_x(pos, a0, a1, a2, a3, keep, send, acc):
    h = pos[3]
    acc[...] = total(a0, a1, a2, a3)
    for i in range(2):
        keep[i] = acc[i, h].astype(BF)
        send[i] = acc[i, 1 - h].astype(BF)


def k_sum_pair(a, b, out, grad):
    both = a[...].astype(F32) + b[...].astype(F32)
    out[...] = both[0].astype(BF)
    grad[...] = both[1].astype(BF)


def place(pos, mask, parts, which, at, out):
    a0, a1, a2, a3 = parts

    def block(s):
        i = at + (s,)
        return total(a0.at[i], a1.at[i], a2.at[i], a3.at[i])

    def store(rr, cc, v):
        out[sub(rr, cc, which)] = v.astype(BF)

    unpack(mask, pos[0] * 4 + pos[1], which, block, store)


def k_place_down(pos, mask, a0, a1, a2, a3, out):
    place(pos, mask, (a0, a1, a2, a3), DOWN, (), out)


def k_place_both(pos, mask, a0, a1, a2, a3, gate, up):
    place(pos, mask, (a0, a1, a2, a3), GATE, (0,), gate)
    place(pos, mask, (a0, a1, a2, a3), UP, (1,), up)


def exchange(value, axis, by, size=4):
    return lax.ppermute(value, axis, [(i, i ^ by) for i in range(size)])


def spread(value, axis):
    return [value] + [exchange(value, axis, j) for j in (1, 2, 3)]


def collect(own, others, axis):
    return [own] + [exchange(v, axis, j) for j, v in zip((1, 2, 3), others)]


def swap(value, flip):
    pairs = [
        ((y * 4 + x) * 2 + h, (x * 4 + y) * 2 + (h ^ flip))
        for y in range(4)
        for x in range(4)
        for h in range(2)
    ]
    return lax.ppermute(value, ("y", "x", "h"), pairs)


def body(tokens, cotangent, gate_weight, up_weight, down_weight, gate_mask, up_mask, down_mask):
    pos = jnp.stack([lax.axis_index(a) for a in ("y", "z", "x", "h", "k")]).astype(jnp.int32)
    mask = jnp.concatenate([gate_mask.T, up_mask.T, down_mask])
    both = jnp.stack([tokens, cotangent])
    pair = jnp.stack([swap(both, 0), swap(both, 1)])
    packed = sds((7, B, B))
    gp, up, dp = call(
        k_pack, (1, 1, 2, 2, 2),
        (pos, mask, gate_weight, up_weight, down_weight), (packed,) * 3,
        (pltpu.VMEM((256, 896), BF), pltpu.VMEM((256, 896), BF), pltpu.VMEM((896, 256), BF),
         pltpu.SemaphoreType.DMA((3,))),
        mib=None,
    )
    dp, pair = lax.optimization_barrier((dp, pair))
    mine = spread(pair, "x")
    dp = lax.all_gather(dp, "z", axis=0)
    gp, dp, mine = lax.optimization_barrier((gp, dp, mine))
    mine = jnp.stack(mine)
    other = exchange(mine, "k", 1, 2)
    gp = lax.all_gather(gp, "z", axis=0)
    acc = pltpu.VMEM((4, B, 896), F32)
    flops = 2 * 512 * 1024 * 896
    blk = (2, B, 896)
    g = call(
        k_grad_gate, (1, 1, 0, 0, 0, 0), (pos, mask, dp, gp, mine, other),
        (sds(blk, F32), sds(blk), sds(blk), sds(blk),
         sds((4, 896, 256)), sds((1024, 896)), sds((512, 1024)), sds((512, 1024))),
        (acc,), flops=2 * flops,
    )
    wd, wg, cot, tok = g[4:]
    g_all = collect(g[0], g[1:4], "y")
    up, _ = lax.optimization_barrier((up, g[1]))
    up = lax.all_gather(up, "z", axis=0)
    up, g_all = lax.optimization_barrier((up, g_all))
    blk = (B, 896)
    u = call(
        k_up, (1, 1, 0, 0), (pos, mask, up, tok),
        (sds(blk, F32), sds(blk), sds(blk), sds(blk), sds((1024, 896))), (acc,), flops=flops,
    )
    wu = u[4]
    u_all = collect(u[0], u[1:4], "y")
    hidden, act = call(k_act, (0,) * 8, (*g_all, *u_all), (sds(blk), sds((2, B, 896))))
    hidden = lax.all_gather(hidden, "y", axis=0)
    hidden, act = lax.optimization_barrier((hidden, act))
    act_all = spread(act, "y")
    blk = (7, B, B)
    e = call(
        k_down_grad, (1, 1, 0, 0), (pos, mask, hidden, cot),
        (sds(blk, F32), sds(blk), sds(blk), sds(blk)),
        (pltpu.VMEM((896, 256), F32),), small=True,
    )
    e_all = collect(e[0], e[1:4], "z")
    act_all, e_all = lax.optimization_barrier((act_all, e_all))
    half, part = (4, 2, 2, B, 256), (2, 2, B, 256)
    act, keep, send = call(
        k_out_in, (1,) + (0,) * 8, (pos, hidden, *act_all, wd, wg, wu),
        (sds((2, 4, B, 896)), sds(half, F32), sds(half)), flops=3 * flops,
    )
    got = exchange(send, "k", 1, 2)
    act, keep = lax.optimization_barrier((act, keep))
    blk = (2, 7, B, B)
    f = call(
        k_weight_grad, (1, 1, 0, 0), (pos, mask, act, tok),
        (sds(blk, F32), sds(blk), sds(blk), sds(blk)),
        (pltpu.VMEM((256, 896), F32),), flops=2 * flops,
    )
    f_all = collect(f[0], f[1:4], "z")
    keep, _ = lax.optimization_barrier((keep, f[1]))
    s = call(
        k_sum_core, (1, 0, 0), (pos, keep, got),
        (sds(part, F32), sds(part), sds(part), sds(part)),
    )
    own, other = call(
        k_sum_x, (1, 0, 0, 0, 0), (pos, *collect(s[0], s[1:], "x")),
        (sds((2, B, 256)), sds((2, B, 256))), (pltpu.VMEM(part, F32),),
    )
    output, input_grad = call(
        k_sum_pair, (0, 0), (swap(own, 0), swap(other, 1)), (sds((B, 256)),) * 2
    )

    spec = (1, 1, 0, 0, 0, 0)
    (down_grad,) = call(k_place_down, spec, (pos, mask, *e_all), (sds((896, 256)),))
    gate_grad, up_grad = call(
        k_place_both, spec, (pos, mask, *f_all), (sds((256, 896)), sds((256, 896)))
    )
    return (output, input_grad, gate_grad, up_grad, down_grad)


def solution(mesh):
    mesh = Mesh(mesh.devices.reshape(4, 4, 4, 2, 2), ("y", "z", "x", "h", "k"))
    row, col = ("y", "z"), ("x", "h", "k")
    return jax.shard_map(
        body,
        mesh=mesh,
        in_specs=(
            P(row, col),
            P(row, col),
            P(row, col),
            P(row, col),
            P(col, row),
            P(None, col),
            P(None, col),
            P(col, None),
        ),
        out_specs=(P(row, col), P(row, col), P(row, col), P(row, col), P(col, row)),
        check_vma=False,
    )
```

```python
import jax
import jax.numpy as jnp
from jax import lax
from jax.experimental import pallas as pl
from jax.experimental.pallas import tpu as pltpu
from jax.sharding import Mesh, PartitionSpec as P

B = 128
VM = pl.BlockSpec(memory_space=pltpu.VMEM)
SM = pl.BlockSpec(memory_space=pltpu.SMEM)
BF = jnp.bfloat16
F32 = jnp.float32


def sds(shape, dtype=BF):
    return jax.ShapeDtypeStruct(shape, dtype)


def call(kernel, specs, args, outs, scratch=(), flops=0, mib=24, small=False):
    nbytes = 0 if small else sum(a.size * a.dtype.itemsize for a in list(args) + list(outs))
    return pl.pallas_call(
        kernel,
        out_shape=tuple(outs),
        in_specs=[(VM, SM, pl.BlockSpec(memory_space=pltpu.HBM))[s] for s in specs],
        out_specs=tuple(VM for _ in outs),
        scratch_shapes=list(scratch),
        compiler_params=pltpu.CompilerParams(vmem_limit_bytes=mib and mib * 1024 * 1024),
        cost_estimate=pl.CostEstimate(flops=flops, bytes_accessed=nbytes, transcendentals=0),
    )(*args)


GATE, UP, DOWN = 0, 7, 14


def cells(mask, tile, which):
    slot = jnp.int32(0)
    for cc in range(7):
        for rr in range(2):
            on = mask[which + cc, 2 * tile + rr]
            yield rr, cc, on == 1, jnp.minimum(slot, 6)
            slot = slot + on
    yield None, None, slot, None


def sub(rr, cc, which):
    a, b = (cc, rr) if which == DOWN else (rr, cc)
    return pl.ds(a * B, B), pl.ds(b * B, B)


def pack(mask, tile, which, source, out, layout=None):
    layout = which if layout is None else layout
    for at, (rr, cc, on, slot) in enumerate(cells(mask, tile, which)):
        if rr is None:
            for p in range(5, 7):

                @pl.when(on <= p)
                def _(p=p):
                    out[p] = jnp.zeros((B, B), out.dtype)

        elif at < 7:
            out[slot] = source[sub(rr, cc, layout)].astype(out.dtype)
        else:

            @pl.when(on)
            def _(rr=rr, cc=cc, slot=slot):
                out[slot] = source[sub(rr, cc, layout)].astype(out.dtype)


def unpack(mask, tile, which, block, store):
    for rr, cc, on, slot in cells(mask, tile, which):
        if rr is not None:
            found = block(slot)
            store(rr, cc, jnp.where(on, found, jnp.zeros_like(found)))


def k_pack(pos, mask, gw, uw, dw, gp, up, dp, gv, uv, dv, sems):
    tile = pos[0] * 4 + pos[1]
    copies = [
        pltpu.make_async_copy(src, dst, sems.at[i])
        for i, (src, dst) in enumerate(((dw, dv), (gw, gv), (uw, uv)))
    ]
    for c in copies:
        c.start()
    copies[0].wait()
    pack(mask, tile, DOWN, dv, dp)
    copies[1].wait()
    pack(mask, tile, GATE, gv, gp)
    copies[2].wait()
    pack(mask, tile, UP, uv, up)


def assemble(pos, mine, other, which, out):
    x, h, k = pos[2], pos[3], pos[4]
    for s in range(4):
        rows = pl.ds(pl.multiple_of(jnp.bitwise_xor(x, s) * B, B), B)
        for a in range(2):
            for b, piece in enumerate((mine, other)):
                q = 2 * jnp.bitwise_xor(h, a) + jnp.bitwise_xor(k, b)
                out[rows, columns(q)] = piece[s, a, which]


def dense_tile_rows(y, mask, which, panel, dense):
    for z in range(4):

        def store(rr, cc, v):
            dense[z * 256 + rr * B : z * 256 + (rr + 1) * B, cc * B : (cc + 1) * B] = v

        unpack(mask, 4 * y + z, which, lambda s: panel[z, s], store)


def shares(y, acc, outs, at=()):
    outs[0][at + (Ellipsis,)] = acc[y]
    for j in (1, 2, 3):
        outs[j][at + (Ellipsis,)] = acc[jnp.bitwise_xor(y, j)].astype(BF)


def k_grad_gate(pos, mask, dp, gp, mine, other, o0, o1, o2, o3, wd, wg, cot, tok, acc):
    y = pos[0]
    for z in range(4):

        def store(rr, cc, v):
            wd[z, cc * B : (cc + 1) * B, rr * B : (rr + 1) * B] = v

        unpack(mask, 4 * y + z, DOWN, lambda s: dp[z, s], store)
    assemble(pos, mine, other, 1, cot)
    got = None
    for q in range(4):
        term = lax.dot_general(
            cot[:, q * 256 : (q + 1) * 256], wd[q], NT, preferred_element_type=F32
        )
        got = term if got is None else got + term
    acc[...] = got.reshape(4, B, 896)
    shares(y, acc, (o0, o1, o2, o3), (0,))
    dense_tile_rows(y, mask, GATE, gp, wg)
    assemble(pos, mine, other, 0, tok)
    got = jnp.dot(tok[...], wg[...], preferred_element_type=F32)
    acc[...] = got.reshape(4, B, 896)
    shares(y, acc, (o0, o1, o2, o3), (1,))


def k_up(pos, mask, panel, tok, o0, o1, o2, o3, dense, acc):
    dense_tile_rows(pos[0], mask, UP, panel, dense)
    got = jnp.dot(tok[...], dense[...], preferred_element_type=F32)
    acc[...] = got.reshape(4, B, 896)
    shares(pos[0], acc, (o0, o1, o2, o3))


def total(own, *others):
    out = own[...]
    for o in others:
        out = out + o[...].astype(F32)
    return out


def k_act(a0, a1, a2, a3, b0, b1, b2, b3, hid, act):
    both = total(a0, a1, a2, a3)
    grad, gate = both[0], both[1]
    up = total(b0, b1, b2, b3)
    sig = jax.nn.sigmoid(gate)
    hid[...] = (gate * sig * up).astype(BF)
    act[0] = (grad * up * sig * (1.0 + gate * (1.0 - sig))).astype(BF)
    act[1] = (grad * (gate * sig)).astype(BF)


def columns(q):
    return pl.ds(pl.multiple_of(q * 256, 256), 256)


TN = (((0,), (0,)), ((), ()))
NT = (((1,), (1,)), ((), ()))


def k_turn(a, b, at, bt):
    at[...] = a[...].T
    bt[...] = b[...].T


def rows_of(q):
    return pl.ds(pl.multiple_of(q * 256, 256), 256)


def k_down_grad(pos, mask, hid, cot_t, d0, d1, d2, d3, acc):
    y, z = pos[0], pos[1]
    right = hid[...].reshape(512, 896)
    for j, out in ((1, d1), (2, d2), (3, d3), (0, d0)):
        zz = jnp.bitwise_xor(z, j)
        acc[...] = jnp.dot(cot_t[rows_of(zz), :], right, preferred_element_type=F32)
        pack(mask, 4 * y + zz, DOWN, acc, out, GATE)


def k_weight_grad(pos, mask, act, tok_t, d0, d1, d2, d3, acc):
    y, z = pos[0], pos[1]
    for half, which in enumerate((GATE, UP)):
        right = act[half].reshape(512, 896)
        for j, out in ((1, d1), (2, d2), (3, d3), (0, d0)):
            zz = jnp.bitwise_xor(z, j)
            acc[...] = jnp.dot(tok_t[rows_of(zz), :], right, preferred_element_type=F32)
            pack(mask, 4 * y + zz, which, acc, out.at[half])


def k_out_in(pos, hid, a0, a1, a2, a3, wd, wg, wu, act, keep, send):
    y, k = pos[0], pos[4]
    for j, a in enumerate((a0, a1, a2, a3)):
        for half in range(2):
            act[half, jnp.bitwise_xor(y, j)] = a[half]
    left = hid[...].reshape(512, 896)
    gact, uact = act[0].reshape(512, 896), act[1].reshape(512, 896)
    for out, kk in ((send, 1 - k), (keep, k)):
        for h in range(2):
            q = 2 * h + kk
            got = jnp.dot(left, wd[q], preferred_element_type=F32)
            out[:, 0, h] = got.reshape(4, B, 256).astype(out.dtype)
            rows = columns(q)
            got = lax.dot_general(gact, wg[rows, :], NT, preferred_element_type=F32)
            got = got + lax.dot_general(uact, wu[rows, :], NT, preferred_element_type=F32)
            out[:, 1, h] = got.reshape(4, B, 256).astype(out.dtype)


def k_sum_core(pos, keep, got, o0, o1, o2, o3):
    x = pos[2]
    for j, out in enumerate((o0, o1, o2, o3)):
        at = jnp.bitwise_xor(x, j)
        out[...] = (keep[at] + got[at].astype(F32)).astype(out.dtype)


def k_sum_x(pos, a0, a1, a2, a3, keep, send, acc):
    h = pos[3]
    acc[...] = total(a0, a1, a2, a3)
    for i in range(2):
        keep[i] = acc[i, h].astype(BF)
        send[i] = acc[i, 1 - h].astype(BF)


def k_sum_pair(a, b, out, grad):
    both = a[...].astype(F32) + b[...].astype(F32)
    out[...] = both[0].astype(BF)
    grad[...] = both[1].astype(BF)


def place(pos, mask, parts, which, at, out):
    a0, a1, a2, a3 = parts

    def block(s):
        i = at + (s,)
        return total(a0.at[i], a1.at[i], a2.at[i], a3.at[i])

    def store(rr, cc, v):
        out[sub(rr, cc, which)] = (v.T if which == DOWN else v).astype(BF)

    unpack(mask, pos[0] * 4 + pos[1], which, block, store)


def k_place_down(pos, mask, a0, a1, a2, a3, out):
    place(pos, mask, (a0, a1, a2, a3), DOWN, (), out)


def k_place_both(pos, mask, a0, a1, a2, a3, gate, up):
    place(pos, mask, (a0, a1, a2, a3), GATE, (0,), gate)
    place(pos, mask, (a0, a1, a2, a3), UP, (1,), up)


def exchange(value, axis, by, size=4):
    return lax.ppermute(value, axis, [(i, i ^ by) for i in range(size)])


def spread(value, axis):
    return [value] + [exchange(value, axis, j) for j in (1, 2, 3)]


def collect(own, others, axis):
    return [own] + [exchange(v, axis, j) for j, v in zip((1, 2, 3), others)]


def swap(value, flip):
    pairs = [
        ((y * 4 + x) * 2 + h, (x * 4 + y) * 2 + (h ^ flip))
        for y in range(4)
        for x in range(4)
        for h in range(2)
    ]
    return lax.ppermute(value, ("y", "x", "h"), pairs)


def body(tokens, cotangent, gate_weight, up_weight, down_weight, gate_mask, up_mask, down_mask):
    pos = jnp.stack([lax.axis_index(a) for a in ("y", "z", "x", "h", "k")]).astype(jnp.int32)
    mask = jnp.concatenate([gate_mask.T, up_mask.T, down_mask])
    both = jnp.stack([tokens, cotangent])
    pair = jnp.stack([swap(both, 0), swap(both, 1)])
    packed = sds((7, B, B))
    gp, up, dp = call(
        k_pack, (1, 1, 2, 2, 2),
        (pos, mask, gate_weight, up_weight, down_weight), (packed,) * 3,
        (pltpu.VMEM((256, 896), BF), pltpu.VMEM((256, 896), BF), pltpu.VMEM((896, 256), BF),
         pltpu.SemaphoreType.DMA((3,))),
        mib=None,
    )
    dp, pair = lax.optimization_barrier((dp, pair))
    mine = spread(pair, "x")
    dp = lax.all_gather(dp, "z", axis=0)
    gp, dp, mine = lax.optimization_barrier((gp, dp, mine))
    mine = jnp.stack(mine)
    other = exchange(mine, "k", 1, 2)
    gp = lax.all_gather(gp, "z", axis=0)
    acc = pltpu.VMEM((4, B, 896), F32)
    flops = 2 * 512 * 1024 * 896
    blk = (2, B, 896)
    g = call(
        k_grad_gate, (1, 1, 0, 0, 0, 0), (pos, mask, dp, gp, mine, other),
        (sds(blk, F32), sds(blk), sds(blk), sds(blk),
         sds((4, 896, 256)), sds((1024, 896)), sds((512, 1024)), sds((512, 1024))),
        (acc,), flops=2 * flops,
    )
    wd, wg, cot, tok = g[4:]
    g_all = collect(g[0], g[1:4], "y")
    up, _ = lax.optimization_barrier((up, g[1]))
    up = lax.all_gather(up, "z", axis=0)
    up, g_all = lax.optimization_barrier((up, g_all))
    blk = (B, 896)
    u = call(
        k_up, (1, 1, 0, 0), (pos, mask, up, tok),
        (sds(blk, F32), sds(blk), sds(blk), sds(blk), sds((1024, 896))), (acc,), flops=flops,
    )
    wu = u[4]
    u_all = collect(u[0], u[1:4], "y")
    cot, tok, _ = lax.optimization_barrier((cot, tok, u[1]))
    cot_t, tok_t = call(k_turn, (0, 0), (cot, tok), (sds((1024, 512)), sds((1024, 512))))
    u_own, cot_t, tok_t = lax.optimization_barrier((u[0], cot_t, tok_t))
    u_all = [u_own] + u_all[1:]
    hidden, act = call(k_act, (0,) * 8, (*g_all, *u_all), (sds(blk), sds((2, B, 896))))
    hidden = lax.all_gather(hidden, "y", axis=0)
    hidden, act = lax.optimization_barrier((hidden, act))
    act_all = spread(act, "y")
    blk = (7, B, B)
    e = call(
        k_down_grad, (1, 1, 0, 0), (pos, mask, hidden, cot_t),
        (sds(blk, F32), sds(blk), sds(blk), sds(blk)),
        (pltpu.VMEM((256, 896), F32),), small=True,
    )
    e_all = collect(e[0], e[1:4], "z")
    act_all, e_all = lax.optimization_barrier((act_all, e_all))
    half, part = (4, 2, 2, B, 256), (2, 2, B, 256)
    act, keep, send = call(
        k_out_in, (1,) + (0,) * 8, (pos, hidden, *act_all, wd, wg, wu),
        (sds((2, 4, B, 896)), sds(half, F32), sds(half)), flops=3 * flops,
    )
    got = exchange(send, "k", 1, 2)
    act, keep = lax.optimization_barrier((act, keep))
    blk = (2, 7, B, B)
    f = call(
        k_weight_grad, (1, 1, 0, 0), (pos, mask, act, tok_t),
        (sds(blk, F32), sds(blk), sds(blk), sds(blk)),
        (pltpu.VMEM((256, 896), F32),), flops=2 * flops,
    )
    f_all = collect(f[0], f[1:4], "z")
    keep, _ = lax.optimization_barrier((keep, f[1]))
    s = call(
        k_sum_core, (1, 0, 0), (pos, keep, got),
        (sds(part, F32), sds(part), sds(part), sds(part)),
    )
    own, other = call(
        k_sum_x, (1, 0, 0, 0, 0), (pos, *collect(s[0], s[1:], "x")),
        (sds((2, B, 256)), sds((2, B, 256))), (pltpu.VMEM(part, F32),),
    )
    output, input_grad = call(
        k_sum_pair, (0, 0), (swap(own, 0), swap(other, 1)), (sds((B, 256)),) * 2
    )

    spec = (1, 1, 0, 0, 0, 0)
    (down_grad,) = call(k_place_down, spec, (pos, mask, *e_all), (sds((896, 256)),))
    gate_grad, up_grad = call(
        k_place_both, spec, (pos, mask, *f_all), (sds((256, 896)), sds((256, 896)))
    )
    return (output, input_grad, gate_grad, up_grad, down_grad)


def solution(mesh):
    mesh = Mesh(mesh.devices.reshape(4, 4, 4, 2, 2), ("y", "z", "x", "h", "k"))
    row, col = ("y", "z"), ("x", "h", "k")
    return jax.shard_map(
        body,
        mesh=mesh,
        in_specs=(
            P(row, col),
            P(row, col),
            P(row, col),
            P(row, col),
            P(col, row),
            P(None, col),
            P(None, col),
            P(col, None),
        ),
        out_specs=(P(row, col), P(row, col), P(row, col), P(row, col), P(col, row)),
        check_vma=False,
    )
```
